256 devices in a mesh: examples: 32 (over y, z), shard: 4 (over x), reps: 2 (over core).
Axes of the slice: x: 4, y: 4, z: 8, core: 2. Of those that a mesh axis runs over, the one named last changes fastest.
Arguments:
- train_inputs: bfloat16 [4096, 8, 4096], P(('examples', 'reps')), may hold values from -10 to 10
- train_grads: bfloat16 [4096, 8, 14336], P(('examples', 'reps'), None, 'shard'), may hold values from -10 to 10
- query_inputs: bfloat16 [128, 8, 4096], P(('examples', 'reps')), may hold values from -10 to 10
- query_grads: bfloat16 [128, 8, 14336], P(('examples', 'reps'), None, 'shard'), may hold values from -10 to 10
- block_maps: bfloat16 [128, 32, 16], replicated, may hold values from -0.125 to 0.125
- block_index: int32 [128], replicated, may hold values from 0 to 1
- block_sign: int32 [128], replicated, may hold values from 0 to 1
- ff_map: bfloat16 [14336, 16], P('shard'), may hold values from -0.09375 to 0.09375
Outputs:
- scores: float32 [4096, 128], P(('examples', 'reps'))
The draws below stay inside these ranges and needn't reach their ends.
All inputs are finite; a program needn't handle non-finite values.
Results may differ from the reference program's by a relative error of at most 0.0003.
Values sent between devices are 32-bit elements; how exact they have to be, the bound alone decides.
No kernel may reach another device: no remote copies, remote signals or barrier semaphores. Data moves between devices by JAX's collectives and lax.ppermute only.
A program may use at most 64 MiB of HBM per device.

```python
import math
import jax
import jax.numpy as jnp
from jax import lax

D = 4096
FF = 14336
NBLOCKS = 128
BLK_ROWS = 32
OUTB = 2
K1 = 32
K2 = 16
RANK = 8
EXAMPLES = 4096
QUERIES = 128
N_SHARD = 4


cluster_count = 32


def cluster_lead(key, member_salt, sign_salt, gain_salt, row_count, col_count):
    member = jax.random.randint(jax.random.fold_in(key, member_salt), (row_count,), 0, cluster_count)
    sign_table = (2 * jax.random.randint(jax.random.fold_in(key, sign_salt), (cluster_count, col_count), 0, 2) - 1).astype(jnp.float32)
    gain_table = jnp.exp(jax.random.uniform(jax.random.fold_in(key, gain_salt), (cluster_count,), jnp.float32, math.log(0.35), math.log(3.5)))
    return sign_table[member] * gain_table[member][:, None]


def factor_rows(key, lead_rows, row_count, col_count):
    first_key, second_key = jax.random.split(key)
    rank_coef = jax.random.truncated_normal(first_key, -2.0, 2.0, (row_count, RANK), jnp.float32)
    noise_part = jax.random.truncated_normal(second_key, -3.0, 3.0, (row_count, RANK, col_count), jnp.float32)
    return (rank_coef[:, :, None] * lead_rows[:, None, :] + noise_part).astype(jnp.bfloat16)


def draw_train_inputs(key, part):
    lead_rows = cluster_lead(key, 101, 201, 301, EXAMPLES, D)
    key = jax.random.fold_in(key, 11)
    return factor_rows(key, lead_rows, EXAMPLES, D)


def draw_train_grads(key, part):
    lead_rows = cluster_lead(key, 101, 202, 302, EXAMPLES, FF)
    key = jax.random.fold_in(key, 12)
    return factor_rows(key, lead_rows, EXAMPLES, FF)


def draw_query_inputs(key, part):
    lead_rows = cluster_lead(key, 102, 201, 301, QUERIES, D)
    key = jax.random.fold_in(key, 13)
    return factor_rows(key, lead_rows, QUERIES, D)


def draw_query_grads(key, part):
    lead_rows = cluster_lead(key, 102, 202, 302, QUERIES, FF)
    key = jax.random.fold_in(key, 14)
    return factor_rows(key, lead_rows, QUERIES, FF)


def touch_ends(result, stream_key, low, top_value):
    longest = result.shape.index(max(result.shape))
    spots = []
    for shift in (0, 1):
        where = [jax.random.randint(jax.random.fold_in(stream_key, axis), (), 0, length) for axis, length in enumerate(result.shape)]
        where[longest] = (where[longest] + shift) % result.shape[longest]
        spots.append(tuple(where))
    return result.at[spots[0]].set(low).at[spots[1]].set(top_value)


def block_scale(key, dims, cuts, smallest, top_value):
    def one(axis_at, blocks):
        steps = jax.random.uniform(jax.random.fold_in(jax.random.fold_in(key, 6), axis_at), (blocks,), jnp.float32, smallest / len(cuts), top_value / len(cuts))
        return jnp.repeat(jnp.exp(steps), dims[axis_at] // blocks).reshape((-1,) + (1,) * (len(dims) - axis_at - 1))

    loudness = one(*cuts[0])
    for cut in cuts[1:]:
        loudness = loudness * one(*cut)
    return loudness


def bell_draw(own_key, shape, deviation, most, cuts=(), kind=jnp.bfloat16):
    loudness = block_scale(own_key, shape, cuts, -0.22, 0.18) if cuts else 1.0
    values = jax.random.normal(own_key, shape, jnp.float32) * deviation * loudness
    return jnp.minimum(jnp.maximum(values, -most), most).astype(kind)


def setup_inputs(seed: int = 0) -> dict:
    keys = jax.random.split(jax.random.key(seed), 9)
    train_inputs = draw_train_inputs(jax.random.fold_in(keys[8], 71), 0)
    train_grads = draw_train_grads(jax.random.fold_in(keys[8], 71), 0)
    query_inputs = draw_query_inputs(jax.random.fold_in(keys[8], 71), 0)
    query_grads = draw_query_grads(jax.random.fold_in(keys[8], 71), 0)
    block_maps = bell_draw(keys[4], (NBLOCKS, BLK_ROWS, K1 // OUTB), (D // OUTB) ** -0.5, 0.125)
    block_index = touch_ends(jax.random.randint(keys[5], (NBLOCKS,), 0, OUTB), jax.random.fold_in(keys[5], 1), 0, OUTB - 1).astype(jnp.int32)
    block_sign = touch_ends(jax.random.randint(keys[6], (NBLOCKS,), 0, 2), jax.random.fold_in(keys[6], 1), 0, 1).astype(jnp.int32)
    ff_map = bell_draw(keys[7], (FF, K2), (FF // N_SHARD) ** -0.5, 0.09375, ((0, 4),))
    return dict(train_inputs=train_inputs, train_grads=train_grads, query_inputs=query_inputs, query_grads=query_grads, block_maps=block_maps, block_index=block_index, block_sign=block_sign, ff_map=ff_map)


ridge_weight = 1.0

def build_map(block_maps, block_index, block_sign):
    chooser = (block_index[:, None] == jnp.arange(OUTB, dtype=jnp.int32)[None, :]).astype(jnp.float32)
    chooser = chooser * (2 * block_sign - 1).astype(jnp.float32)[:, None]
    dense = block_maps.astype(jnp.float32)[:, :, None, :] * chooser[:, None, :, None]
    return dense.reshape(D, K1).astype(jnp.bfloat16)

def left_side(inputs, input_map):
    row_count = inputs.shape[0]
    flat = inputs.reshape(row_count * RANK, D)
    return jnp.dot(flat.astype(jnp.float32), input_map.astype(jnp.float32), preferred_element_type=jnp.float32).reshape(row_count, RANK, K1)

def right_side(grad_rows, ff_part):
    row_count = grad_rows.shape[0]
    flat = grad_rows.reshape(row_count * RANK, grad_rows.shape[2])
    return jnp.dot(flat.astype(jnp.float32), ff_part.astype(jnp.float32), preferred_element_type=jnp.float32).reshape(row_count, RANK, K2)

def combine(left_part, right_part):
    outer = jnp.einsum('erk,erl->ekl', left_part, right_part, precision=lax.Precision.HIGHEST)
    return outer.reshape(left_part.shape[0], K1 * K2) / math.sqrt(RANK)

def reference(train_inputs, train_grads, query_inputs, query_grads, block_maps, block_index, block_sign, ff_map):
    input_map = build_map(block_maps, block_index, block_sign)
    train_left = left_side(train_inputs, input_map)
    query_left = left_side(query_inputs, input_map)
    width = FF // N_SHARD
    identity = jnp.eye(K1 * K2, dtype=jnp.float32)
    gathered = jnp.zeros((train_inputs.shape[0], query_inputs.shape[0]), jnp.float32)
    for shard_idx in range(N_SHARD):
        ff_part = ff_map[shard_idx * width:(shard_idx + 1) * width]
        train_feats = combine(train_left, right_side(train_grads[:, :, shard_idx * width:(shard_idx + 1) * width], ff_part))
        query_feats = combine(query_left, right_side(query_grads[:, :, shard_idx * width:(shard_idx + 1) * width], ff_part))
        gram = jnp.dot(train_feats.T, train_feats, precision=lax.Precision.HIGHEST) / EXAMPLES + ridge_weight * identity
        lower_factor = jnp.linalg.cholesky(gram)
        solved = jax.scipy.linalg.cho_solve((lower_factor, True), query_feats.T)
        gathered = gathered + jnp.dot(train_feats, solved, precision=lax.Precision.HIGHEST)
    return gathered / math.sqrt(K1 * K2 * N_SHARD)
```

```python
import math

import jax
import jax.numpy as jnp
from jax import lax
from jax.experimental import pallas as pl
from jax.experimental.pallas import tpu as pltpu
from jax.sharding import PartitionSpec as P

D = 4096
OUTB = 2
K1 = 32
K2 = 16
KB = 512
RANK = 8
EXAMPLES = 4096
RIDGE = 1.0
TILE = 128
PANEL = 16
NB = KB // TILE
PAIRS = [(i, j) for i in range(NB) for j in range(i, NB)]
HALF = len(PAIRS) // 2
NY = 4
NZ = 8
CHUNK = HALF * TILE // NY
HIGH = lax.Precision.HIGHEST
VMEM_LIMIT = 48 << 20


def dot(a, b, contract=(1, 0)):
    return lax.dot_general(
        a,
        b,
        (((contract[0],), (contract[1],)), ((), ())),
        precision=HIGH,
        preferred_element_type=jnp.float32,
    )


def move(block, axis, target):
    count = lax.axis_size(axis)
    return lax.ppermute(block, axis, [(i, target(i)) for i in range(count)])


def along_y(block, step):
    return move(block, "examples", lambda e: (e // NZ + step) % NY * NZ + e % NZ)


def along_z(block, step):
    return move(block, "examples", lambda e: e // NZ * NZ + (e % NZ + step) % NZ)


def build_map(block_maps, block_index, block_sign):
    chooser = (block_index[:, None] == jnp.arange(OUTB, dtype=jnp.int32)[None, :]).astype(
        jnp.float32
    )
    chooser = chooser * (2 * block_sign - 1).astype(jnp.float32)[:, None]
    dense = block_maps.astype(jnp.float32)[:, :, None, :] * chooser[:, None, :, None]
    return dense.reshape(D, K1).astype(jnp.bfloat16)


def features(inputs, grad_rows, input_map, ff_part):
    row_count = inputs.shape[0]
    left_part = jnp.dot(
        inputs.reshape(row_count * RANK, D), input_map, preferred_element_type=jnp.float32
    )
    right_part = jnp.dot(
        grad_rows.reshape(row_count * RANK, grad_rows.shape[2]),
        ff_part,
        preferred_element_type=jnp.float32,
    )
    outer = jnp.einsum(
        "erk,erl->ekl",
        left_part.reshape(row_count, RANK, K1),
        right_part.reshape(row_count, RANK, K2),
        precision=HIGH,
    )
    return outer.reshape(row_count, K1 * K2) / math.sqrt(RANK)


def lookup(table, index):
    value = jnp.int32(table[0])
    for place, entry in enumerate(table[1:], 1):
        value = jnp.where(index == place, jnp.int32(entry), value)
    return value


def gram_kernel(own_ref, other_ref, keep_ref, first_ref, second_ref, third_ref, half):
    rep = lax.axis_index("reps")
    y = lax.axis_index("examples") // NZ
    for place in range(HALF):
        low, high = PAIRS[place], PAIRS[HALF + place]
        row = pl.multiple_of(jnp.where(rep == 0, low[0], high[0]) * TILE, TILE)
        col = pl.multiple_of(jnp.where(rep == 0, low[1], high[1]) * TILE, TILE)
        total = dot(own_ref[:, pl.ds(row, TILE)], own_ref[:, pl.ds(col, TILE)], (0, 0))
        total += dot(other_ref[:, pl.ds(row, TILE)], other_ref[:, pl.ds(col, TILE)], (0, 0))
        half[place * TILE : (place + 1) * TILE, :] = total * (1.0 / EXAMPLES)
    for step, out_ref in enumerate((keep_ref, first_ref, second_ref, third_ref)):
        start = pl.multiple_of(lax.rem(y + step, NY) * CHUNK, 8)
        out_ref[...] = half[pl.ds(start, CHUNK), :]


def panel_inverse(rows, first):
    lane = lax.broadcasted_iota(jnp.int32, (PANEL, TILE), 1)
    row = lax.broadcasted_iota(jnp.int32, (PANEL, TILE), 0)
    spread = [
        jnp.broadcast_to(rows[:, first + j : first + j + 1], (PANEL, TILE)) for j in range(PANEL)
    ]
    inside = (lane >= first) & (lane < first + PANEL)
    rows = jnp.where(inside, (lane - first == row).astype(jnp.float32), rows)
    for j in range(PANEL):
        scale = 1.0 / spread[j][j : j + 1, :]
        pivot_row = rows[j : j + 1, :] * scale
        rows = jnp.where(row == j, pivot_row, rows - spread[j] * pivot_row)
        for k in range(j + 1, PANEL):
            part = spread[k][j : j + 1, :] * scale
            spread[k] = jnp.where(row == j, part, spread[k] - spread[j] * part)
    return rows


def block_inverse(block):
    lane = lax.broadcasted_iota(jnp.int32, (TILE, TILE), 1)
    for first in range(0, TILE, PANEL):
        last = first + PANEL
        fresh = panel_inverse(block[first:last], first)
        update = dot(block[:, first:last], fresh)
        block = jnp.where((lane >= first) & (lane < last), 0.0, block) - update
        parts = [block[:first]] if first else []
        parts.append(fresh)
        if last < TILE:
            parts.append(block[last:])
        block = jnp.concatenate(parts, 0)
    return block


def solve_kernel(own_ref, other_ref, feats_ref, out_ref, gram, query):
    rep = lax.axis_index("reps")
    spot = lax.axis_index("examples")
    y, z = spot // NZ, lax.rem(spot, NZ)
    piece = own_ref.shape[0] // NY
    query_rows = piece - CHUNK
    for side, ref in enumerate((own_ref, other_ref)):
        holder = rep if side == 0 else 1 - rep
        for step in range(NY):
            source = lax.rem(y + NY - step, NY)
            start = pl.multiple_of(holder * (HALF * TILE) + source * CHUNK, 8)
            gram[pl.ds(start, CHUNK), :] = ref[step * piece : step * piece + CHUNK, :]
            at = (side * NY + step) * query_rows
            query[at : at + query_rows, :] = ref[step * piece + CHUNK : (step + 1) * piece, :]

    total_rows = 2 * NY * query_rows
    r = lax.broadcasted_iota(jnp.int32, (total_rows, TILE), 0)
    n = lax.broadcasted_iota(jnp.int32, (total_rows, TILE), 1)
    side, step = r >> 8, (r >> 6) & 3
    group, pair, item, part = (r >> 4) & 3, (r >> 3) & 1, (r >> 2) & 1, r & 3
    shift = jnp.where(group == 0, 0, jnp.where(group == 1, 6, jnp.where(group == 2, 2, 4)))
    source_z = ((z + shift) & 7) ^ pair
    source_y = (y + 4 - step) & 3
    source = (((source_y * NZ + source_z) * 2 + (side ^ rep)) * 2) + item
    values = query[...]
    right = [
        dot(values, ((source == n) & (part == c)).astype(jnp.float32), (0, 0)) for c in range(NB)
    ]

    eye = (
        lax.broadcasted_iota(jnp.int32, (TILE, TILE), 0)
        == lax.broadcasted_iota(jnp.int32, (TILE, TILE), 1)
    ).astype(jnp.float32) * RIDGE
    block = {}
    for place, (i, j) in enumerate(PAIRS):
        value = gram[place * TILE : (place + 1) * TILE, :]
        block[i, j] = value + eye if i == j else value

    solved = []
    for b in range(NB):
        inverse = block_inverse(block[b, b])
        wide = jnp.concatenate([block[b, j] for j in range(b + 1, NB)] + [right[b]], 1)
        done = dot(inverse, wide)
        solved.append(done)
        for i in range(b + 1, NB):
            change = dot(block[b, i], done[:, (i - b - 1) * TILE :], (0, 0))
            for j in range(i, NB):
                block[i, j] = block[i, j] - change[:, (j - i) * TILE : (j - i + 1) * TILE]
            right[i] = right[i] - change[:, (NB - i) * TILE :]
    answer = [None] * NB
    for b in reversed(range(NB)):
        value = solved[b][:, (NB - 1 - b) * TILE :]
        if b < NB - 1:
            later = jnp.concatenate(answer[b + 1 :], 0)
            value = value - dot(solved[b][:, : (NB - 1 - b) * TILE], later)
        answer[b] = value
    out_ref[...] = dot(feats_ref[...], jnp.concatenate(answer, 0)) * (1.0 / math.sqrt(4 * KB))


def on_device(
    train_inputs,
    train_grads,
    query_inputs,
    query_grads,
    block_maps,
    block_index,
    block_sign,
    ff_map,
):
    input_map = build_map(block_maps, block_index, block_sign)
    train_feats = features(train_inputs, train_grads, input_map, ff_map)
    query_feats = features(query_inputs, query_grads, input_map, ff_map)
    other_feats = move(train_feats, "reps", lambda r: 1 - r)
    params = pltpu.CompilerParams(vmem_limit_bytes=VMEM_LIMIT)
    piece = jax.ShapeDtypeStruct((CHUNK, TILE), jnp.float32)
    keep, first, second, third = pl.pallas_call(
        gram_kernel,
        out_shape=[piece] * NY,
        scratch_shapes=[pltpu.VMEM((HALF * TILE, TILE), jnp.float32)],
        compiler_params=params,
    )(train_feats, other_feats)
    second = along_y(second, 2)
    first = along_y(first, 1)
    third = along_y(third, 3)
    gram = keep + first + second + third
    held = jnp.concatenate([gram, query_feats.reshape(-1, TILE)], 0)
    near = move(held, "examples", lambda e: e ^ 1)
    held = jnp.concatenate([gram + near[:CHUNK], held[CHUNK:], near[CHUNK:]], 0)
    far = along_z(held, 4)
    left = along_z(held, 2)
    right = along_z(held, 6)
    gram = held[:CHUNK] + left[:CHUNK] + right[:CHUNK] + far[:CHUNK]
    held = jnp.concatenate([gram, held[CHUNK:], left[CHUNK:], right[CHUNK:], far[CHUNK:]], 0)
    second = along_y(held, 2)
    first = along_y(held, 1)
    third = along_y(held, 3)
    mine = jnp.concatenate([held, first, second, third], 0)
    theirs = move(mine, "reps", lambda r: 1 - r)
    value = pl.pallas_call(
        solve_kernel,
        out_shape=jax.ShapeDtypeStruct((train_feats.shape[0], TILE), jnp.float32),
        scratch_shapes=[
            pltpu.VMEM((len(PAIRS) * TILE, TILE), jnp.float32),
            pltpu.VMEM((KB, TILE), jnp.float32),
        ],
        compiler_params=params,
    )(mine, theirs, train_feats)
    second = move(value, "shard", lambda s: s ^ 2)
    first = move(value, "shard", lambda s: s ^ 1)
    third = move(value, "shard", lambda s: s ^ 3)
    return (value + first) + (second + third)


def solution(mesh):
    placed = (
        P(("examples", "reps"), None, None),
        P(("examples", "reps"), None, "shard"),
        P(("examples", "reps"), None, None),
        P(("examples", "reps"), None, "shard"),
        P(),
        P(),
        P(),
        P("shard", None),
    )
    return jax.shard_map(
        on_device,
        mesh=mesh,
        in_specs=placed,
        out_specs=P(("examples", "reps"), None),
        check_vma=False,
    )
```

```python
import math

import jax
import jax.numpy as jnp
from jax import lax
from jax.experimental import pallas as pl
from jax.experimental.pallas import tpu as pltpu
from jax.sharding import PartitionSpec as P

D = 4096
K1 = 32
K2 = 16
KB = 512
RANK = 8
EXAMPLES = 4096
NBLOCKS = 128
BLOCK_ROWS = 32
CHUNKS = 1
PARTS = 2
LATER = 8
RIDGE = 1.0
TILE = 128
PANEL = 16
NB = KB // TILE
PAIRS = [(i, j) for i in range(NB) for j in range(i, NB)]
HALF = len(PAIRS) // 2
NY = 4
NZ = 8
CHUNK = HALF * TILE // NY
HIGH = lax.Precision.HIGHEST
VMEM_LIMIT = 48 << 20
VMEM_WHOLE = 40 << 20


def dot(a, b, contract=(1, 0)):
    return lax.dot_general(
        a,
        b,
        (((contract[0],), (contract[1],)), ((), ())),
        precision=HIGH,
        preferred_element_type=jnp.float32,
    )


def move(block, axis, target):
    count = lax.axis_size(axis)
    return lax.ppermute(block, axis, [(i, target(i)) for i in range(count)])


def along_y(block, step):
    return move(block, "examples", lambda e: (e // NZ + step) % NY * NZ + e % NZ)


def along_z(block, step):
    return move(block, "examples", lambda e: e // NZ * NZ + (e % NZ + step) % NZ)


def split(value):
    high = value.astype(jnp.bfloat16)
    rest = value - high.astype(jnp.float32)
    middle = rest.astype(jnp.bfloat16)
    return high, middle, (rest - middle.astype(jnp.float32)).astype(jnp.bfloat16)


def spread_parts(value):
    high, middle, low = (part.astype(jnp.float32) for part in split(value))
    first = high + pltpu.roll(middle, 64, 1)
    return jnp.concatenate([first, low], 1).astype(jnp.bfloat16)


def feature_kernel(*refs):
    sources, feats_ref, query_ref = refs[:8], refs[8], refs[9]
    index_ref, sign_ref, maps_ref, ff_ref, grads_ref, inputs_ref = refs[10:16]
    dense, weights, ff_weights, total, right_total, arrived = refs[16:]
    index_hbm, sign_hbm, maps_hbm, ff_hbm, query_grads_hbm, grads_hbm, query_hbm, inputs_hbm = sources
    main = inputs_hbm.shape[0]
    rows = inputs_ref.shape[0]
    plan = [
        (index_hbm, index_ref),
        (sign_hbm, sign_ref),
        (ff_hbm, ff_ref),
        (maps_hbm, maps_ref),
        (query_grads_hbm, grads_ref.at[main:rows, :]),
        (grads_hbm, grads_ref.at[0:main, :]),
        (query_hbm, inputs_ref.at[main:rows, :]),
    ]
    width = inputs_ref.shape[1] // CHUNKS
    for k in range(CHUNKS):
        part = slice(k * width, (k + 1) * width)
        plan.append((inputs_hbm.at[:, part], inputs_ref.at[0:main, part]))
    copies = [
        pltpu.make_async_copy(source, target, arrived.at[k])
        for k, (source, target) in enumerate(plan)
    ]
    for copy in copies[:6]:
        copy.start()

    def iota(shape, axis):
        return lax.broadcasted_iota(jnp.int32, shape, axis)

    for copy in copies[:3]:
        copy.wait()
    place = (iota((K2, TILE), 1) - K1 == iota((K2, TILE), 0)).astype(jnp.bfloat16)
    ff_weights[...] = lax.dot_general(
        ff_ref[...], place, (((0,), (0,)), ((), ())), preferred_element_type=jnp.float32
    ).astype(jnp.bfloat16)

    copies[3].wait()
    signs = 2 * sign_ref[...] - 1
    chooser = [
        jnp.where(index_ref[...] == c, signs, 0).astype(jnp.float32) for c in range(K1 // K2)
    ]
    groups = TILE // K1
    group = iota((NBLOCKS, TILE), 1) // K1
    for first in range(0, BLOCK_ROWS, groups):
        if first == LATER:
            for copy in copies[6:]:
                copy.start()
        stack = []
        for i in range(first, first + groups):
            values = maps_ref[i].astype(jnp.float32)
            stack += [values * factor for factor in chooser]
        turned = jnp.concatenate(stack, 0).T
        for g in range(groups):
            dense[pl.ds(first + g, NBLOCKS, stride=BLOCK_ROWS), :] = jnp.where(
                group == g, turned, 0.0
            )
    weights[...] = dense[...].astype(jnp.bfloat16)

    def project(values_ref, weights_ref, out_ref):
        depth = values_ref.shape[1] // PARTS

        def body(k, carry):
            part = pl.ds(pl.multiple_of(k * depth, TILE), depth)
            out_ref[...] += jnp.dot(
                values_ref[:, part], weights_ref[part, :], preferred_element_type=jnp.float32
            )
            return carry

        out_ref[...] = jnp.zeros_like(out_ref)
        lax.fori_loop(0, PARTS, body, 0)

    copies[4].wait()
    copies[5].wait()
    project(grads_ref, ff_weights, right_total)
    for copy in copies[6:]:
        copy.wait()
    project(inputs_ref, weights, total)
    left = total[...]
    left = left + pltpu.roll(left, 2 * K1, 1)
    left = left + pltpu.roll(left, K1, 1)
    total[...] = jnp.where(iota((rows, TILE), 1) < K1, left, right_total[...])

    source = iota((2 * TILE, 2 * KB), 0) & 63
    lanes = iota((2 * TILE, 2 * KB), 1)
    from_left = (lanes < KB) & (source == lanes // K2)
    from_right = (lanes >= KB) & (source == K1 + (lanes & (K2 - 1)))
    used = iota((2 * TILE, 2 * KB), 0) < 3 * 64
    expand = ((from_left | from_right) & used).astype(jnp.bfloat16)
    count = feats_ref.shape[0]
    by_rank = [total[pl.ds(r, count, stride=RANK), :] for r in range(RANK)]
    by_rank.append(total[main:rows, :])
    wide = jnp.dot(
        spread_parts(jnp.concatenate(by_rank, 0)), expand, preferred_element_type=jnp.float32
    )
    product = wide[:, :KB] * wide[:, KB:]
    value = product[:count]
    for r in range(1, RANK):
        value = value + product[r * count : (r + 1) * count]
    feats_ref[...] = value * (1.0 / math.sqrt(RANK))
    for i in range((rows - main) // RANK):
        first = main + i * RANK
        row = jnp.sum(product[first : first + RANK], 0, keepdims=True) * (1.0 / math.sqrt(RANK))
        for c in range(NB):
            at = 2 * c + i
            query_ref[at : at + 1, :] = row[:, c * TILE : (c + 1) * TILE]


def features(train, grads, query, query_grads, block_maps, block_index, block_sign, ff_map):
    count = train.shape[0]
    train, grads, query, query_grads = (
        x.reshape(-1, x.shape[-1]) for x in (train, grads, query, query_grads)
    )
    operands = [
        block_index.reshape(1, -1),
        block_sign.reshape(1, -1),
        block_maps.transpose(1, 2, 0),
        ff_map.T,
        query_grads,
        grads,
        query,
        train,
    ]
    rows = train.shape[0] + query.shape[0]
    return pl.pallas_call(
        feature_kernel,
        in_specs=[pl.BlockSpec(memory_space=pltpu.HBM)] * len(operands),
        out_shape=[
            jax.ShapeDtypeStruct((count, KB), jnp.float32),
            jax.ShapeDtypeStruct((2 * NB, TILE), jnp.float32),
        ],
        scratch_shapes=[pltpu.VMEM(x.shape, x.dtype) for x in operands[:4]]
        + [
            pltpu.VMEM((rows, grads.shape[1]), jnp.bfloat16),
            pltpu.VMEM((rows, D), jnp.bfloat16),
            pltpu.VMEM((D, TILE), jnp.float32),
            pltpu.VMEM((D, TILE), jnp.bfloat16),
            pltpu.VMEM((grads.shape[1], TILE), jnp.bfloat16),
            pltpu.VMEM((rows, TILE), jnp.float32),
            pltpu.VMEM((rows, TILE), jnp.float32),
            pltpu.SemaphoreType.DMA((7 + CHUNKS,)),
        ],
        compiler_params=pltpu.CompilerParams(vmem_limit_bytes=VMEM_WHOLE),
    )(*[pltpu.with_memory_space_constraint(x, pltpu.HBM) for x in operands])


def gram_kernel(own_ref, other_ref, keep_ref, first_ref, second_ref, third_ref, half):
    rep = lax.axis_index("reps")
    y = lax.axis_index("examples") // NZ
    for place in range(HALF):
        low, high = PAIRS[place], PAIRS[HALF + place]
        row = pl.multiple_of(jnp.where(rep == 0, low[0], high[0]) * TILE, TILE)
        col = pl.multiple_of(jnp.where(rep == 0, low[1], high[1]) * TILE, TILE)
        total = dot(own_ref[:, pl.ds(row, TILE)], own_ref[:, pl.ds(col, TILE)], (0, 0))
        total += dot(other_ref[:, pl.ds(row, TILE)], other_ref[:, pl.ds(col, TILE)], (0, 0))
        half[place * TILE : (place + 1) * TILE, :] = total * (1.0 / EXAMPLES)
    for step, out_ref in enumerate((keep_ref, first_ref, second_ref, third_ref)):
        start = pl.multiple_of(lax.rem(y + step, NY) * CHUNK, 8)
        out_ref[...] = half[pl.ds(start, CHUNK), :]


def panel_inverse(rows, first):
    lane = lax.broadcasted_iota(jnp.int32, (PANEL, TILE), 1)
    row = lax.broadcasted_iota(jnp.int32, (PANEL, TILE), 0)
    spread = [
        jnp.broadcast_to(rows[:, first + j : first + j + 1], (PANEL, TILE)) for j in range(PANEL)
    ]
    inside = (lane >= first) & (lane < first + PANEL)
    rows = jnp.where(inside, (lane - first == row).astype(jnp.float32), rows)
    for j in range(PANEL):
        scale = 1.0 / spread[j][j : j + 1, :]
        pivot_row = rows[j : j + 1, :] * scale
        rows = jnp.where(row == j, pivot_row, rows - spread[j] * pivot_row)
        for k in range(j + 1, PANEL):
            part = spread[k][j : j + 1, :] * scale
            spread[k] = jnp.where(row == j, part, spread[k] - spread[j] * part)
    return rows


def panel_update(rows, factors, first, fresh):
    lane = lax.broadcasted_iota(jnp.int32, (PANEL, TILE), 1)
    inside = (lane >= first) & (lane < first + PANEL)
    even, odd = jnp.where(inside, 0.0, rows), None
    for j in range(PANEL):
        column = jnp.broadcast_to(factors[:, first + j : first + j + 1], (PANEL, TILE))
        term = column * fresh[j : j + 1]
        if j % 2 == 0:
            even = even - term
        else:
            odd = term if odd is None else odd + term
    return even - odd


def block_inverse(block, between=lambda: None):
    lane = lax.broadcasted_iota(jnp.int32, (PANEL, TILE), 1)
    count = TILE // PANEL
    rows = [block[i * PANEL : (i + 1) * PANEL] for i in range(count)]
    fresh = None
    for t in range(count):
        first = t * PANEL
        current = rows[t]
        if t:
            current = panel_update(current, current, first - PANEL, fresh)
        fresh = panel_inverse(current, first)
        others = [i for i in range(count) if i not in (t, t + 1)]
        factors = jnp.concatenate([rows[i] for i in others], 0)[:, first : first + PANEL]
        update = dot(factors, fresh)
        inside = (lane >= first) & (lane < first + PANEL)
        for k, i in enumerate(others):
            rows[i] = jnp.where(inside, 0.0, rows[i]) - update[k * PANEL : (k + 1) * PANEL]
        rows[t] = fresh
        between()
    return jnp.concatenate(rows, 0)


def solve_kernel(own_ref, other_ref, feats_ref, out_ref, gram, query):
    rep = lax.axis_index("reps")
    spot = lax.axis_index("examples")
    y, z = spot // NZ, lax.rem(spot, NZ)
    piece = own_ref.shape[0] // NY
    query_rows = piece - CHUNK
    for side, ref in enumerate((own_ref, other_ref)):
        holder = rep if side == 0 else 1 - rep
        for step in range(NY):
            source = lax.rem(y + NY - step, NY)
            start = pl.multiple_of(holder * (HALF * TILE) + source * CHUNK, 8)
            gram[pl.ds(start, CHUNK), :] = ref[step * piece : step * piece + CHUNK, :]
            at = (side * NY + step) * query_rows
            query[at : at + query_rows, :] = ref[step * piece + CHUNK : (step + 1) * piece, :]

    total_rows = 2 * NY * query_rows
    r = lax.broadcasted_iota(jnp.int32, (total_rows, TILE), 0)
    n = lax.broadcasted_iota(jnp.int32, (total_rows, TILE), 1)
    side, step = r >> 8, (r >> 6) & 3
    group, pair, part, item = (r >> 4) & 3, (r >> 3) & 1, (r >> 1) & 3, r & 1
    shift = jnp.where(group == 0, 0, jnp.where(group == 1, 6, jnp.where(group == 2, 2, 4)))
    source_z = ((z + shift) & 7) ^ pair
    source_y = (y + 4 - step) & 3
    source = (((source_y * NZ + source_z) * 2 + (side ^ rep)) * 2) + item
    right = [None] * NB

    def pick(c):
        chosen = ((source == n) & (part == c)).astype(jnp.bfloat16)
        right[c] = sum(
            lax.dot_general(
                piece, chosen, (((0,), (0,)), ((), ())), preferred_element_type=jnp.float32
            )
            for piece in split(query[...])
        )

    eye = (
        lax.broadcasted_iota(jnp.int32, (TILE, TILE), 0)
        == lax.broadcasted_iota(jnp.int32, (TILE, TILE), 1)
    ).astype(jnp.float32) * RIDGE
    block = {}
    for place, (i, j) in enumerate(PAIRS):
        value = gram[place * TILE : (place + 1) * TILE, :]
        block[i, j] = value + eye if i == j else value

    solved = []
    pending = [lambda c=c: pick(c) for c in range(NB)]

    def between():
        if pending:
            pending.pop(0)()

    for b in range(NB):
        inverse = block_inverse(block[b, b], between)
        while pending:
            between()
        if b == NB - 1:
            solved.append([dot(inverse, right[b])])
            break
        near = dot(inverse, block[b, b + 1])
        block[b + 1, b + 1] = block[b + 1, b + 1] - dot(block[b, b + 1], near, (0, 0))
        done = [near]
        solved.append(done)

        def finish(b=b, done=done, inverse=inverse):
            width = NB - 2 - b
            wide = jnp.concatenate([block[b, j] for j in range(b + 2, NB)] + [right[b]], 1)
            wide = dot(inverse, wide)
            done += [wide[:, k * TILE : (k + 1) * TILE] for k in range(width + 1)]

        def trail(i, b=b, done=done):
            first = max(i, b + 2)
            change = dot(block[b, i], jnp.concatenate(done[first - b - 1 :], 1), (0, 0))
            for j in range(first, NB):
                at = (j - first) * TILE
                block[i, j] = block[i, j] - change[:, at : at + TILE]
            right[i] = right[i] - change[:, (NB - first) * TILE :]

        pending.append(finish)
        for i in range(b + 1, NB):
            pending.append(lambda i=i, trail=trail: trail(i))
    answer = [None] * NB
    for b in reversed(range(NB)):
        value = solved[b][NB - 1 - b]
        if b < NB - 1:
            later = jnp.concatenate(answer[b + 1 :], 0)
            value = value - dot(jnp.concatenate(solved[b][: NB - 1 - b], 1), later)
        answer[b] = value
    out_ref[...] = dot(feats_ref[...], jnp.concatenate(answer, 0)) * (1.0 / math.sqrt(4 * KB))


def on_device(
    train_inputs,
    train_grads,
    query_inputs,
    query_grads,
    block_maps,
    block_index,
    block_sign,
    ff_map,
):
    train_feats, query_feats = features(
        train_inputs,
        train_grads,
        query_inputs,
        query_grads,
        block_maps,
        block_index,
        block_sign,
        ff_map,
    )
    other_feats = move(train_feats, "reps", lambda r: 1 - r)
    params = pltpu.CompilerParams(vmem_limit_bytes=VMEM_LIMIT)
    piece = jax.ShapeDtypeStruct((CHUNK, TILE), jnp.float32)
    keep, first, second, third = pl.pallas_call(
        gram_kernel,
        out_shape=[piece] * NY,
        scratch_shapes=[pltpu.VMEM((HALF * TILE, TILE), jnp.float32)],
        compiler_params=params,
    )(train_feats, other_feats)
    second = along_y(second, 2)
    first = along_y(first, 1)
    third = along_y(third, 3)
    gram = keep + first + second + third
    held = jnp.concatenate([gram, query_feats], 0)
    near = move(held, "examples", lambda e: e ^ 1)
    held = jnp.concatenate([gram + near[:CHUNK], held[CHUNK:], near[CHUNK:]], 0)
    far = along_z(held, 4)
    left = along_z(held, 2)
    right = along_z(held, 6)
    gram = held[:CHUNK] + left[:CHUNK] + right[:CHUNK] + far[:CHUNK]
    held = jnp.concatenate([gram, held[CHUNK:], left[CHUNK:], right[CHUNK:], far[CHUNK:]], 0)
    second = along_y(held, 2)
    first = along_y(held, 1)
    third = along_y(held, 3)
    mine = jnp.concatenate([held, first, second, third], 0)
    theirs = move(mine, "reps", lambda r: 1 - r)
    value = pl.pallas_call(
        solve_kernel,
        out_shape=jax.ShapeDtypeStruct((train_feats.shape[0], TILE), jnp.float32),
        scratch_shapes=[
            pltpu.VMEM((len(PAIRS) * TILE, TILE), jnp.float32),
            pltpu.VMEM((KB, TILE), jnp.float32),
        ],
        compiler_params=params,
    )(mine, theirs, train_feats)
    second = move(value, "shard", lambda s: s ^ 2)
    first = move(value, "shard", lambda s: s ^ 1)
    third = move(value, "shard", lambda s: s ^ 3)
    return (value + first) + (second + third)


def solution(mesh):
    placed = (
        P(("examples", "reps"), None, None),
        P(("examples", "reps"), None, "shard"),
        P(("examples", "reps"), None, None),
        P(("examples", "reps"), None, "shard"),
        P(),
        P(),
        P(),
        P("shard", None),
    )
    return jax.shard_map(
        on_device,
        mesh=mesh,
        in_specs=placed,
        out_specs=P(("examples", "reps"), None),
        check_vma=False,
    )
```

```python
import math

import jax
import jax.numpy as jnp
from jax import lax
from jax.experimental import pallas as pl
from jax.experimental.pallas import tpu as pltpu
from jax.sharding import PartitionSpec as P

D = 4096
K1 = 32
K2 = 16
KB = 512
RANK = 8
EXAMPLES = 4096
NBLOCKS = 128
BLOCK_ROWS = 32
CHUNKS = 1
PARTS = 2
LATER = 8
RIDGE = 1.0
TILE = 128
PANEL = 16
NB = KB // TILE
NY = 4
NZ = 8
SIDES = [(0, 1), (0, 2), (0, 3)], [(1, 2), (1, 3), (2, 3)]
CHUNK = TILE + 8
HIGH = lax.Precision.HIGHEST
VMEM_LIMIT = 48 << 20
VMEM_WHOLE = 40 << 20


def dot(a, b, contract=(1, 0)):
    return lax.dot_general(
        a,
        b,
        (((contract[0],), (contract[1],)), ((), ())),
        precision=HIGH,
        preferred_element_type=jnp.float32,
    )


def move(block, axis, target):
    count = lax.axis_size(axis)
    return lax.ppermute(block, axis, [(i, target(i)) for i in range(count)])


def along_y(block, step):
    return move(block, "examples", lambda e: (e // NZ + step) % NY * NZ + e % NZ)


def along_z(block, step):
    return move(block, "examples", lambda e: e // NZ * NZ + (e % NZ + step) % NZ)


def split(value):
    high = value.astype(jnp.bfloat16)
    rest = value - high.astype(jnp.float32)
    middle = rest.astype(jnp.bfloat16)
    return high, middle, (rest - middle.astype(jnp.float32)).astype(jnp.bfloat16)


def spread_parts(value):
    high, middle, low = (part.astype(jnp.float32) for part in split(value))
    first = high + pltpu.roll(middle, 64, 1)
    return jnp.concatenate([first, low], 1).astype(jnp.bfloat16)


def feature_kernel(*refs):
    sources, feats_ref, query_ref = refs[:8], refs[8], refs[9]
    index_ref, sign_ref, maps_ref, ff_ref, grads_ref, inputs_ref = refs[10:16]
    dense, weights, ff_weights, total, right_total, arrived = refs[16:]
    index_hbm, sign_hbm, maps_hbm, ff_hbm, query_grads_hbm, grads_hbm, query_hbm, inputs_hbm = sources
    main = inputs_hbm.shape[0]
    rows = inputs_ref.shape[0]
    plan = [
        (index_hbm, index_ref),
        (sign_hbm, sign_ref),
        (ff_hbm, ff_ref),
        (maps_hbm, maps_ref),
        (query_grads_hbm, grads_ref.at[main:rows, :]),
        (grads_hbm, grads_ref.at[0:main, :]),
        (query_hbm, inputs_ref.at[main:rows, :]),
    ]
    width = inputs_ref.shape[1] // CHUNKS
    for k in range(CHUNKS):
        part = slice(k * width, (k + 1) * width)
        plan.append((inputs_hbm.at[:, part], inputs_ref.at[0:main, part]))
    copies = [
        pltpu.make_async_copy(source, target, arrived.at[k])
        for k, (source, target) in enumerate(plan)
    ]
    for copy in copies[:6]:
        copy.start()

    def iota(shape, axis):
        return lax.broadcasted_iota(jnp.int32, shape, axis)

    for copy in copies[:3]:
        copy.wait()
    place = (iota((K2, TILE), 1) - K1 == iota((K2, TILE), 0)).astype(jnp.bfloat16)
    ff_weights[...] = lax.dot_general(
        ff_ref[...], place, (((0,), (0,)), ((), ())), preferred_element_type=jnp.float32
    ).astype(jnp.bfloat16)

    copies[3].wait()
    signs = 2 * sign_ref[...] - 1
    chooser = [
        jnp.where(index_ref[...] == c, signs, 0).astype(jnp.float32) for c in range(K1 // K2)
    ]
    groups = TILE // K1
    group = iota((NBLOCKS, TILE), 1) // K1
    for first in range(0, BLOCK_ROWS, groups):
        if first == LATER:
            for copy in copies[6:]:
                copy.start()
        stack = []
        for i in range(first, first + groups):
            values = maps_ref[i].astype(jnp.float32)
            stack += [values * factor for factor in chooser]
        turned = jnp.concatenate(stack, 0).T
        for g in range(groups):
            dense[pl.ds(first + g, NBLOCKS, stride=BLOCK_ROWS), :] = jnp.where(
                group == g, turned, 0.0
            )
    weights[...] = dense[...].astype(jnp.bfloat16)

    def project(values_ref, weights_ref, out_ref):
        depth = values_ref.shape[1] // PARTS

        def body(k, carry):
            part = pl.ds(pl.multiple_of(k * depth, TILE), depth)
            out_ref[...] += jnp.dot(
                values_ref[:, part], weights_ref[part, :], preferred_element_type=jnp.float32
            )
            return carry

        out_ref[...] = jnp.zeros_like(out_ref)
        lax.fori_loop(0, PARTS, body, 0)

    copies[4].wait()
    copies[5].wait()
    project(grads_ref, ff_weights, right_total)
    for copy in copies[6:]:
        copy.wait()
    project(inputs_ref, weights, total)
    left = total[...]
    left = left + pltpu.roll(left, 2 * K1, 1)
    left = left + pltpu.roll(left, K1, 1)
    total[...] = jnp.where(iota((rows, TILE), 1) < K1, left, right_total[...])

    source = iota((2 * TILE, 2 * KB), 0) & 63
    lanes = iota((2 * TILE, 2 * KB), 1)
    from_left = (lanes < KB) & (source == lanes // K2)
    from_right = (lanes >= KB) & (source == K1 + (lanes & (K2 - 1)))
    used = iota((2 * TILE, 2 * KB), 0) < 3 * 64
    expand = ((from_left | from_right) & used).astype(jnp.bfloat16)
    count = feats_ref.shape[0]
    by_rank = [total[pl.ds(r, count, stride=RANK), :] for r in range(RANK)]
    by_rank.append(total[main:rows, :])
    wide = jnp.dot(
        spread_parts(jnp.concatenate(by_rank, 0)), expand, preferred_element_type=jnp.float32
    )
    product = wide[:, :KB] * wide[:, KB:]
    value = product[:count]
    for r in range(1, RANK):
        value = value + product[r * count : (r + 1) * count]
    feats_ref[...] = value * (1.0 / math.sqrt(RANK))
    for i in range((rows - main) // RANK):
        first = main + i * RANK
        row = jnp.sum(product[first : first + RANK], 0, keepdims=True) * (1.0 / math.sqrt(RANK))
        for c in range(NB):
            at = 2 * c + i
            query_ref[at : at + 1, :] = row[:, c * TILE : (c + 1) * TILE]


def features(train, grads, query, query_grads, block_maps, block_index, block_sign, ff_map):
    count = train.shape[0]
    train, grads, query, query_grads = (
        x.reshape(-1, x.shape[-1]) for x in (train, grads, query, query_grads)
    )
    operands = [
        block_index.reshape(1, -1),
        block_sign.reshape(1, -1),
        block_maps.transpose(1, 2, 0),
        ff_map.T,
        query_grads,
        grads,
        query,
        train,
    ]
    rows = train.shape[0] + query.shape[0]
    return pl.pallas_call(
        feature_kernel,
        in_specs=[pl.BlockSpec(memory_space=pltpu.HBM)] * len(operands),
        out_shape=[
            jax.ShapeDtypeStruct((count, KB), jnp.float32),
            jax.ShapeDtypeStruct((2 * NB, TILE), jnp.float32),
        ],
        scratch_shapes=[pltpu.VMEM(x.shape, x.dtype) for x in operands[:4]]
        + [
            pltpu.VMEM((rows, grads.shape[1]), jnp.bfloat16),
            pltpu.VMEM((rows, D), jnp.bfloat16),
            pltpu.VMEM((D, TILE), jnp.float32),
            pltpu.VMEM((D, TILE), jnp.bfloat16),
            pltpu.VMEM((grads.shape[1], TILE), jnp.bfloat16),
            pltpu.VMEM((rows, TILE), jnp.float32),
            pltpu.VMEM((rows, TILE), jnp.float32),
            pltpu.SemaphoreType.DMA((7 + CHUNKS,)),
        ],
        compiler_params=pltpu.CompilerParams(vmem_limit_bytes=VMEM_WHOLE),
    )(*[pltpu.with_memory_space_constraint(x, pltpu.HBM) for x in operands])


def gram_kernel(own_ref, other_ref, keep_ref, first_ref, second_ref, third_ref, half):
    rep = lax.axis_index("reps")
    y = lax.axis_index("examples") // NZ

    def product(low, high):
        row = pl.multiple_of(jnp.where(rep == 0, low[0], high[0]) * TILE, TILE)
        col = pl.multiple_of(jnp.where(rep == 0, low[1], high[1]) * TILE, TILE)
        total = dot(own_ref[:, pl.ds(row, TILE)], own_ref[:, pl.ds(col, TILE)], (0, 0))
        total += dot(other_ref[:, pl.ds(row, TILE)], other_ref[:, pl.ds(col, TILE)], (0, 0))
        return total * (1.0 / EXAMPLES)

    row = lax.broadcasted_iota(jnp.int32, (TILE, TILE), 0)
    col = lax.broadcasted_iota(jnp.int32, (TILE, TILE), 1)
    upper, lower = product((0, 0), (2, 2)), product((1, 1), (3, 3))
    half[...] = jnp.zeros_like(half)
    half[:TILE, :] = jnp.where(row <= col, upper, lower)
    half[TILE : TILE + 1, :] = jnp.sum(jnp.where(row == col, lower, 0.0), 0, keepdims=True)
    for place, (low, high) in enumerate(zip(*SIDES), 1):
        half[place * CHUNK : place * CHUNK + TILE, :] = product(low, high)
    for step, out_ref in enumerate((keep_ref, first_ref, second_ref, third_ref)):
        start = pl.multiple_of(lax.rem(y + step, NY) * CHUNK, 8)
        out_ref[...] = half[pl.ds(start, CHUNK), :]


def panel_inverse(rows, first):
    lane = lax.broadcasted_iota(jnp.int32, (PANEL, TILE), 1)
    row = lax.broadcasted_iota(jnp.int32, (PANEL, TILE), 0)
    spread = [
        jnp.broadcast_to(rows[:, first + j : first + j + 1], (PANEL, TILE)) for j in range(PANEL)
    ]
    inside = (lane >= first) & (lane < first + PANEL)
    rows = jnp.where(inside, (lane - first == row).astype(jnp.float32), rows)
    for j in range(PANEL):
        scale = 1.0 / spread[j][j : j + 1, :]
        pivot_row = rows[j : j + 1, :] * scale
        rows = jnp.where(row == j, pivot_row, rows - spread[j] * pivot_row)
        for k in range(j + 1, PANEL):
            part = spread[k][j : j + 1, :] * scale
            spread[k] = jnp.where(row == j, part, spread[k] - spread[j] * part)
    return rows


def panel_update(rows, factors, first, fresh):
    lane = lax.broadcasted_iota(jnp.int32, (PANEL, TILE), 1)
    inside = (lane >= first) & (lane < first + PANEL)
    even, odd = jnp.where(inside, 0.0, rows), None
    for j in range(PANEL):
        column = jnp.broadcast_to(factors[:, first + j : first + j + 1], (PANEL, TILE))
        term = column * fresh[j : j + 1]
        if j % 2 == 0:
            even = even - term
        else:
            odd = term if odd is None else odd + term
    return even - odd


def block_inverse(block, between=lambda: None):
    lane = lax.broadcasted_iota(jnp.int32, (PANEL, TILE), 1)
    count = TILE // PANEL
    rows = [block[i * PANEL : (i + 1) * PANEL] for i in range(count)]
    fresh = None
    for t in range(count):
        first = t * PANEL
        current = rows[t]
        if t:
            current = panel_update(current, current, first - PANEL, fresh)
        fresh = panel_inverse(current, first)
        others = [i for i in range(count) if i not in (t, t + 1)]
        factors = jnp.concatenate([rows[i] for i in others], 0)[:, first : first + PANEL]
        update = dot(factors, fresh)
        inside = (lane >= first) & (lane < first + PANEL)
        for k, i in enumerate(others):
            rows[i] = jnp.where(inside, 0.0, rows[i]) - update[k * PANEL : (k + 1) * PANEL]
        rows[t] = fresh
        between()
    return jnp.concatenate(rows, 0)


def solve_kernel(*refs):
    pieces, (feats_ref, out_ref, gram, query) = refs[: 2 * NY], refs[2 * NY :]
    rep = lax.axis_index("reps")
    spot = lax.axis_index("examples")
    y, z = spot // NZ, lax.rem(spot, NZ)
    query_rows = pieces[0].shape[0] - CHUNK
    for place, ref in enumerate(pieces):
        holder = rep if place < NY else 1 - rep
        source = lax.rem(y + NY - place % NY, NY)
        start = pl.multiple_of((holder * NY + source) * CHUNK, 8)
        gram[pl.ds(start, CHUNK), :] = ref[:CHUNK, :]
        query[place * query_rows : (place + 1) * query_rows, :] = ref[CHUNK:, :]

    total_rows = 2 * NY * query_rows
    r = lax.broadcasted_iota(jnp.int32, (total_rows, TILE), 0)
    n = lax.broadcasted_iota(jnp.int32, (total_rows, TILE), 1)
    side, step = r >> 8, (r >> 6) & 3
    group, pair, part, item = (r >> 4) & 3, (r >> 3) & 1, (r >> 1) & 3, r & 1
    shift = jnp.where(group == 0, 0, jnp.where(group == 1, 6, jnp.where(group == 2, 2, 4)))
    source_z = ((z + shift) & 7) ^ pair
    source_y = (y + 4 - step) & 3
    source = (((source_y * NZ + source_z) * 2 + (side ^ rep)) * 2) + item
    right = [None] * NB

    def pick(c):
        chosen = ((source == n) & (part == c)).astype(jnp.bfloat16)
        right[c] = sum(
            lax.dot_general(
                piece, chosen, (((0,), (0,)), ((), ())), preferred_element_type=jnp.float32
            )
            for piece in split(query[...])
        )

    row = lax.broadcasted_iota(jnp.int32, (TILE, TILE), 0)
    col = lax.broadcasted_iota(jnp.int32, (TILE, TILE), 1)
    ridge = jnp.where(row == col, RIDGE, 0.0)
    block = {}
    for core, pairs in enumerate(SIDES):
        first = core * NY * CHUNK
        packed = gram[first : first + TILE, :]
        above = jnp.where(row < col, packed, 0.0)
        block[2 * core, 2 * core] = jnp.where(row <= col, packed, above.T) + ridge
        below = jnp.where(row > col, packed, 0.0)
        diagonal = gram[first + TILE : first + TILE + 1, :]
        other = jnp.where(row > col, packed, jnp.where(row == col, diagonal, below.T))
        block[2 * core + 1, 2 * core + 1] = other + ridge
        for place, pair in enumerate(pairs, 1):
            start = first + place * CHUNK
            block[pair] = gram[start : start + TILE, :]

    solved = []
    pending = [lambda c=c: pick(c) for c in range(NB)]

    def between():
        if pending:
            pending.pop(0)()

    for b in range(NB):
        inverse = block_inverse(block[b, b], between)
        while pending:
            between()
        if b == NB - 1:
            solved.append([dot(inverse, right[b])])
            break
        near = dot(inverse, block[b, b + 1])
        block[b + 1, b + 1] = block[b + 1, b + 1] - dot(block[b, b + 1], near, (0, 0))
        done = [near]
        solved.append(done)

        def finish(b=b, done=done, inverse=inverse):
            width = NB - 2 - b
            wide = jnp.concatenate([block[b, j] for j in range(b + 2, NB)] + [right[b]], 1)
            wide = dot(inverse, wide)
            done += [wide[:, k * TILE : (k + 1) * TILE] for k in range(width + 1)]

        def trail(i, b=b, done=done):
            first = max(i, b + 2)
            change = dot(block[b, i], jnp.concatenate(done[first - b - 1 :], 1), (0, 0))
            for j in range(first, NB):
                at = (j - first) * TILE
                block[i, j] = block[i, j] - change[:, at : at + TILE]
            right[i] = right[i] - change[:, (NB - first) * TILE :]

        pending.append(finish)
        for i in range(b + 1, NB):
            pending.append(lambda i=i, trail=trail: trail(i))
    answer = [None] * NB
    for b in reversed(range(NB)):
        value = solved[b][NB - 1 - b]
        if b < NB - 1:
            later = jnp.concatenate(answer[b + 1 :], 0)
            value = value - dot(jnp.concatenate(solved[b][: NB - 1 - b], 1), later)
        answer[b] = value
    out_ref[...] = dot(feats_ref[...], jnp.concatenate(answer, 0)) * (1.0 / math.sqrt(4 * KB))


def on_device(
    train_inputs,
    train_grads,
    query_inputs,
    query_grads,
    block_maps,
    block_index,
    block_sign,
    ff_map,
):
    train_feats, query_feats = features(
        train_inputs,
        train_grads,
        query_inputs,
        query_grads,
        block_maps,
        block_index,
        block_sign,
        ff_map,
    )
    other_feats = move(train_feats, "reps", lambda r: 1 - r)
    params = pltpu.CompilerParams(vmem_limit_bytes=VMEM_LIMIT)
    piece = jax.ShapeDtypeStruct((CHUNK, TILE), jnp.float32)
    keep, first, second, third = pl.pallas_call(
        gram_kernel,
        out_shape=[piece] * NY,
        scratch_shapes=[pltpu.VMEM((NY * CHUNK, TILE), jnp.float32)],
        compiler_params=params,
    )(train_feats, other_feats)
    second = along_y(second, 2)
    first = along_y(first, 1)
    third = along_y(third, 3)
    gram = keep + first + second + third
    held = jnp.concatenate([gram, query_feats], 0)
    near = move(held, "examples", lambda e: e ^ 1)
    held = jnp.concatenate([gram + near[:CHUNK], held[CHUNK:], near[CHUNK:]], 0)
    far = along_z(held, 4)
    left = along_z(held, 2)
    right = along_z(held, 6)
    gram = held[:CHUNK] + left[:CHUNK] + right[:CHUNK] + far[:CHUNK]
    held = jnp.concatenate([gram, held[CHUNK:], left[CHUNK:], right[CHUNK:], far[CHUNK:]], 0)
    second = along_y(held, 2)
    first = along_y(held, 1)
    third = along_y(held, 3)
    mine = [held, first, second, third]
    theirs = [move(piece, "reps", lambda r: 1 - r) for piece in mine]
    value = pl.pallas_call(
        solve_kernel,
        out_shape=jax.ShapeDtypeStruct((train_feats.shape[0], TILE), jnp.float32),
        scratch_shapes=[
            pltpu.VMEM((2 * NY * CHUNK, TILE), jnp.float32),
            pltpu.VMEM((KB, TILE), jnp.float32),
        ],
        compiler_params=params,
    )(*mine, *theirs, train_feats)
    second = move(value, "shard", lambda s: s ^ 2)
    first = move(value, "shard", lambda s: s ^ 1)
    third = move(value, "shard", lambda s: s ^ 3)
    return (value + first) + (second + third)


def solution(mesh):
    placed = (
        P(("examples", "reps"), None, None),
        P(("examples", "reps"), None, "shard"),
        P(("examples", "reps"), None, None),
        P(("examples", "reps"), None, "shard"),
        P(),
        P(),
        P(),
        P("shard", None),
    )
    return jax.shard_map(
        on_device,
        mesh=mesh,
        in_specs=placed,
        out_specs=P(("examples", "reps"), None),
        check_vma=False,
    )
```

```python
import math

import jax
import jax.numpy as jnp
from jax import lax
from jax.experimental import pallas as pl
from jax.experimental.pallas import tpu as pltpu
from jax.sharding import PartitionSpec as P

D = 4096
K1 = 32
K2 = 16
KB = 512
RANK = 8
EXAMPLES = 4096
NBLOCKS = 128
BLOCK_ROWS = 32
CHUNKS = 1
PARTS = 2
LATER = 8
RIDGE = 1.0
TILE = 128
PANEL = 16
NB = KB // TILE
NY = 4
NZ = 8
SIDES = [(0, 1), (0, 2), (0, 3)], [(1, 2), (1, 3), (2, 3)]
CHUNK = TILE + 8
HIGH = lax.Precision.HIGHEST
VMEM_LIMIT = 48 << 20
VMEM_WHOLE = 40 << 20


def dot(a, b, contract=(1, 0)):
    return lax.dot_general(
        a,
        b,
        (((contract[0],), (contract[1],)), ((), ())),
        precision=HIGH,
        preferred_element_type=jnp.float32,
    )


def short_dot(a, b):
    a_high, a_low, _ = split(a)
    b_high, b_low, _ = split(b)
    terms = ((a_low, b_high), (a_high, b_low), (a_high, b_high))
    return sum(jnp.dot(x, y, preferred_element_type=jnp.float32) for x, y in terms)


def move(block, axis, target):
    count = lax.axis_size(axis)
    return lax.ppermute(block, axis, [(i, target(i)) for i in range(count)])


def along_y(block, step):
    return move(block, "examples", lambda e: (e // NZ + step) % NY * NZ + e % NZ)


def along_z(block, step):
    return move(block, "examples", lambda e: e // NZ * NZ + (e % NZ + step) % NZ)


def split(value):
    high = value.astype(jnp.bfloat16)
    rest = value - high.astype(jnp.float32)
    middle = rest.astype(jnp.bfloat16)
    return high, middle, (rest - middle.astype(jnp.float32)).astype(jnp.bfloat16)


def spread_parts(value):
    high, middle, low = (part.astype(jnp.float32) for part in split(value))
    first = high + pltpu.roll(middle, 64, 1)
    return jnp.concatenate([first, low], 1).astype(jnp.bfloat16)


def feature_kernel(*refs):
    sources, feats_ref, query_ref = refs[:8], refs[8], refs[9]
    index_ref, sign_ref, maps_ref, ff_ref, grads_ref, inputs_ref = refs[10:16]
    dense, weights, ff_weights, total, right_total, arrived = refs[16:]
    index_hbm, sign_hbm, maps_hbm, ff_hbm, query_grads_hbm, grads_hbm, query_hbm, inputs_hbm = sources
    main = inputs_hbm.shape[0]
    rows = inputs_ref.shape[0]
    plan = [
        (index_hbm, index_ref),
        (sign_hbm, sign_ref),
        (ff_hbm, ff_ref),
        (maps_hbm, maps_ref),
        (query_grads_hbm, grads_ref.at[main:rows, :]),
        (grads_hbm, grads_ref.at[0:main, :]),
        (query_hbm, inputs_ref.at[main:rows, :]),
    ]
    width = inputs_ref.shape[1] // CHUNKS
    for k in range(CHUNKS):
        part = slice(k * width, (k + 1) * width)
        plan.append((inputs_hbm.at[:, part], inputs_ref.at[0:main, part]))
    copies = [
        pltpu.make_async_copy(source, target, arrived.at[k])
        for k, (source, target) in enumerate(plan)
    ]
    for copy in copies[:6]:
        copy.start()

    def iota(shape, axis):
        return lax.broadcasted_iota(jnp.int32, shape, axis)

    for copy in copies[:3]:
        copy.wait()
    place = (iota((K2, TILE), 1) - K1 == iota((K2, TILE), 0)).astype(jnp.bfloat16)
    ff_weights[...] = lax.dot_general(
        ff_ref[...], place, (((0,), (0,)), ((), ())), preferred_element_type=jnp.float32
    ).astype(jnp.bfloat16)

    copies[3].wait()
    signs = 2 * sign_ref[...] - 1
    chooser = [
        jnp.where(index_ref[...] == c, signs, 0).astype(jnp.float32) for c in range(K1 // K2)
    ]
    groups = TILE // K1
    group = iota((NBLOCKS, TILE), 1) // K1
    for first in range(0, BLOCK_ROWS, groups):
        if first == LATER:
            for copy in copies[6:]:
                copy.start()
        stack = []
        for i in range(first, first + groups):
            values = maps_ref[i].astype(jnp.float32)
            stack += [values * factor for factor in chooser]
        turned = jnp.concatenate(stack, 0).T
        for g in range(groups):
            dense[pl.ds(first + g, NBLOCKS, stride=BLOCK_ROWS), :] = jnp.where(
                group == g, turned, 0.0
            )
    weights[...] = dense[...].astype(jnp.bfloat16)

    def project(values_ref, weights_ref, out_ref):
        depth = values_ref.shape[1] // PARTS

        def body(k, carry):
            part = pl.ds(pl.multiple_of(k * depth, TILE), depth)
            out_ref[...] += jnp.dot(
                values_ref[:, part], weights_ref[part, :], preferred_element_type=jnp.float32
            )
            return carry

        out_ref[...] = jnp.zeros_like(out_ref)
        lax.fori_loop(0, PARTS, body, 0)

    copies[4].wait()
    copies[5].wait()
    project(grads_ref, ff_weights, right_total)
    for copy in copies[6:]:
        copy.wait()
    project(inputs_ref, weights, total)
    left = total[...]
    left = left + pltpu.roll(left, 2 * K1, 1)
    left = left + pltpu.roll(left, K1, 1)
    total[...] = jnp.where(iota((rows, TILE), 1) < K1, left, right_total[...])

    source = iota((2 * TILE, 2 * KB), 0) & 63
    lanes = iota((2 * TILE, 2 * KB), 1)
    from_left = (lanes < KB) & (source == lanes // K2)
    from_right = (lanes >= KB) & (source == K1 + (lanes & (K2 - 1)))
    used = iota((2 * TILE, 2 * KB), 0) < 3 * 64
    expand = ((from_left | from_right) & used).astype(jnp.bfloat16)
    count = feats_ref.shape[0]
    by_rank = [total[pl.ds(r, count, stride=RANK), :] for r in range(RANK)]
    by_rank.append(total[main:rows, :])
    wide = jnp.dot(
        spread_parts(jnp.concatenate(by_rank, 0)), expand, preferred_element_type=jnp.float32
    )
    product = wide[:, :KB] * wide[:, KB:]
    value = product[:count]
    for r in range(1, RANK):
        value = value + product[r * count : (r + 1) * count]
    feats_ref[...] = value * (1.0 / math.sqrt(RANK))
    for i in range((rows - main) // RANK):
        first = main + i * RANK
        row = jnp.sum(product[first : first + RANK], 0, keepdims=True) * (1.0 / math.sqrt(RANK))
        for c in range(NB):
            at = 2 * c + i
            query_ref[at : at + 1, :] = row[:, c * TILE : (c + 1) * TILE]


def features(train, grads, query, query_grads, block_maps, block_index, block_sign, ff_map):
    count = train.shape[0]
    train, grads, query, query_grads = (
        x.reshape(-1, x.shape[-1]) for x in (train, grads, query, query_grads)
    )
    operands = [
        block_index.reshape(1, -1),
        block_sign.reshape(1, -1),
        block_maps.transpose(1, 2, 0),
        ff_map.T,
        query_grads,
        grads,
        query,
        train,
    ]
    rows = train.shape[0] + query.shape[0]
    return pl.pallas_call(
        feature_kernel,
        in_specs=[pl.BlockSpec(memory_space=pltpu.HBM)] * len(operands),
        out_shape=[
            jax.ShapeDtypeStruct((count, KB), jnp.float32),
            jax.ShapeDtypeStruct((2 * NB, TILE), jnp.float32),
        ],
        scratch_shapes=[pltpu.VMEM(x.shape, x.dtype) for x in operands[:4]]
        + [
            pltpu.VMEM((rows, grads.shape[1]), jnp.bfloat16),
            pltpu.VMEM((rows, D), jnp.bfloat16),
            pltpu.VMEM((D, TILE), jnp.float32),
            pltpu.VMEM((D, TILE), jnp.bfloat16),
            pltpu.VMEM((grads.shape[1], TILE), jnp.bfloat16),
            pltpu.VMEM((rows, TILE), jnp.float32),
            pltpu.VMEM((rows, TILE), jnp.float32),
            pltpu.SemaphoreType.DMA((7 + CHUNKS,)),
        ],
        compiler_params=pltpu.CompilerParams(vmem_limit_bytes=VMEM_WHOLE),
    )(*[pltpu.with_memory_space_constraint(x, pltpu.HBM) for x in operands])


def gram_kernel(own_ref, other_ref, keep_ref, first_ref, second_ref, third_ref, half):
    rep = lax.axis_index("reps")
    y = lax.axis_index("examples") // NZ

    def product(low, high):
        row = pl.multiple_of(jnp.where(rep == 0, low[0], high[0]) * TILE, TILE)
        col = pl.multiple_of(jnp.where(rep == 0, low[1], high[1]) * TILE, TILE)
        total = dot(own_ref[:, pl.ds(row, TILE)], own_ref[:, pl.ds(col, TILE)], (0, 0))
        total += dot(other_ref[:, pl.ds(row, TILE)], other_ref[:, pl.ds(col, TILE)], (0, 0))
        return total * (1.0 / EXAMPLES)

    row = lax.broadcasted_iota(jnp.int32, (TILE, TILE), 0)
    col = lax.broadcasted_iota(jnp.int32, (TILE, TILE), 1)
    upper, lower = product((0, 0), (2, 2)), product((1, 1), (3, 3))
    half[...] = jnp.zeros_like(half)
    half[:TILE, :] = jnp.where(row <= col, upper, lower)
    half[TILE : TILE + 1, :] = jnp.sum(jnp.where(row == col, lower, 0.0), 0, keepdims=True)
    for place, (low, high) in enumerate(zip(*SIDES), 1):
        half[place * CHUNK : place * CHUNK + TILE, :] = product(low, high)
    for step, out_ref in enumerate((keep_ref, first_ref, second_ref, third_ref)):
        start = pl.multiple_of(lax.rem(y + step, NY) * CHUNK, 8)
        out_ref[...] = half[pl.ds(start, CHUNK), :]


def panel_inverse(rows, first):
    lane = lax.broadcasted_iota(jnp.int32, (PANEL, TILE), 1)
    row = lax.broadcasted_iota(jnp.int32, (PANEL, TILE), 0)
    spread = [
        jnp.broadcast_to(rows[:, first + j : first + j + 1], (PANEL, TILE)) for j in range(PANEL)
    ]
    inside = (lane >= first) & (lane < first + PANEL)
    rows = jnp.where(inside, (lane - first == row).astype(jnp.float32), rows)
    for j in range(PANEL):
        scale = 1.0 / spread[j][j : j + 1, :]
        pivot_row = rows[j : j + 1, :] * scale
        rows = jnp.where(row == j, pivot_row, rows - spread[j] * pivot_row)
        for k in range(j + 1, PANEL):
            part = spread[k][j : j + 1, :] * scale
            spread[k] = jnp.where(row == j, part, spread[k] - spread[j] * part)
    return rows


def panel_update(rows, factors, first, fresh):
    lane = lax.broadcasted_iota(jnp.int32, (PANEL, TILE), 1)
    inside = (lane >= first) & (lane < first + PANEL)
    even, odd = jnp.where(inside, 0.0, rows), None
    for j in range(PANEL):
        column = jnp.broadcast_to(factors[:, first + j : first + j + 1], (PANEL, TILE))
        term = column * fresh[j : j + 1]
        if j % 2 == 0:
            even = even - term
        else:
            odd = term if odd is None else odd + term
    return even - odd


def block_inverse(block, between=lambda: None):
    lane = lax.broadcasted_iota(jnp.int32, (PANEL, TILE), 1)
    count = TILE // PANEL
    rows = [block[i * PANEL : (i + 1) * PANEL] for i in range(count)]
    fresh = None
    for t in range(count):
        first = t * PANEL
        current = rows[t]
        if t:
            current = panel_update(current, current, first - PANEL, fresh)
        fresh = panel_inverse(current, first)
        others = [i for i in range(count) if i not in (t, t + 1)]
        factors = jnp.concatenate([rows[i] for i in others], 0)[:, first : first + PANEL]
        update = dot(factors, fresh)
        inside = (lane >= first) & (lane < first + PANEL)
        for k, i in enumerate(others):
            rows[i] = jnp.where(inside, 0.0, rows[i]) - update[k * PANEL : (k + 1) * PANEL]
        rows[t] = fresh
        between()
    return jnp.concatenate(rows, 0)


def solve_kernel(*refs):
    pieces, (feats_ref, out_ref, gram, query) = refs[: 2 * NY], refs[2 * NY :]
    rep = lax.axis_index("reps")
    spot = lax.axis_index("examples")
    y, z = spot // NZ, lax.rem(spot, NZ)
    query_rows = pieces[0].shape[0] - CHUNK
    for place, ref in enumerate(pieces):
        holder = rep if place < NY else 1 - rep
        source = lax.rem(y + NY - place % NY, NY)
        start = pl.multiple_of((holder * NY + source) * CHUNK, 8)
        gram[pl.ds(start, CHUNK), :] = ref[:CHUNK, :]
        query[place * query_rows : (place + 1) * query_rows, :] = ref[CHUNK:, :]

    total_rows = 2 * NY * query_rows
    r = lax.broadcasted_iota(jnp.int32, (total_rows, TILE), 0)
    n = lax.broadcasted_iota(jnp.int32, (total_rows, TILE), 1)
    side, step = r >> 8, (r >> 6) & 3
    group, pair, part, item = (r >> 4) & 3, (r >> 3) & 1, (r >> 1) & 3, r & 1
    shift = jnp.where(group == 0, 0, jnp.where(group == 1, 6, jnp.where(group == 2, 2, 4)))
    source_z = ((z + shift) & 7) ^ pair
    source_y = (y + 4 - step) & 3
    source = (((source_y * NZ + source_z) * 2 + (side ^ rep)) * 2) + item
    right = [None] * NB

    def pick(c):
        chosen = ((source == n) & (part == c)).astype(jnp.bfloat16)
        right[c] = sum(
            lax.dot_general(
                piece, chosen, (((0,), (0,)), ((), ())), preferred_element_type=jnp.float32
            )
            for piece in split(query[...])
        )

    row = lax.broadcasted_iota(jnp.int32, (TILE, TILE), 0)
    col = lax.broadcasted_iota(jnp.int32, (TILE, TILE), 1)
    ridge = jnp.where(row == col, RIDGE, 0.0)
    block = {}
    for core, pairs in enumerate(SIDES):
        first = core * NY * CHUNK
        packed = gram[first : first + TILE, :]
        above = jnp.where(row < col, packed, 0.0)
        block[2 * core, 2 * core] = jnp.where(row <= col, packed, above.T) + ridge
        below = jnp.where(row > col, packed, 0.0)
        diagonal = gram[first + TILE : first + TILE + 1, :]
        other = jnp.where(row > col, packed, jnp.where(row == col, diagonal, below.T))
        block[2 * core + 1, 2 * core + 1] = other + ridge
        for place, pair in enumerate(pairs, 1):
            start = first + place * CHUNK
            block[pair] = gram[start : start + TILE, :]

    solved = []
    pending = [lambda c=c: pick(c) for c in range(NB)]

    def between():
        if pending:
            pending.pop(0)()

    for b in range(NB):
        inverse = block_inverse(block[b, b], between)
        while pending:
            between()
        if b == NB - 1:
            solved.append([dot(inverse, right[b])])
            break
        near = dot(inverse, block[b, b + 1])
        block[b + 1, b + 1] = block[b + 1, b + 1] - dot(block[b, b + 1], near, (0, 0))
        done = [near]
        solved.append(done)

        def finish(b=b, done=done, inverse=inverse):
            width = NB - 2 - b
            wide = jnp.concatenate([block[b, j] for j in range(b + 2, NB)] + [right[b]], 1)
            wide = dot(inverse, wide)
            done += [wide[:, k * TILE : (k + 1) * TILE] for k in range(width + 1)]

        def trail(i, b=b, done=done):
            first = max(i, b + 2)
            change = dot(block[b, i], jnp.concatenate(done[first - b - 1 :], 1), (0, 0))
            for j in range(first, NB):
                at = (j - first) * TILE
                block[i, j] = block[i, j] - change[:, at : at + TILE]
            right[i] = right[i] - change[:, (NB - first) * TILE :]

        pending.append(finish)
        for i in range(b + 1, NB):
            pending.append(lambda i=i, trail=trail: trail(i))
    answer = [None] * NB
    for b in reversed(range(NB)):
        value = solved[b][NB - 1 - b]
        if b < NB - 1:
            later = jnp.concatenate(answer[b + 1 :], 0)
            value = value - short_dot(jnp.concatenate(solved[b][: NB - 1 - b], 1), later)
        answer[b] = value
    out_ref[...] = short_dot(feats_ref[...], jnp.concatenate(answer, 0)) * (1.0 / math.sqrt(4 * KB))


def on_device(
    train_inputs,
    train_grads,
    query_inputs,
    query_grads,
    block_maps,
    block_index,
    block_sign,
    ff_map,
):
    train_feats, query_feats = features(
        train_inputs,
        train_grads,
        query_inputs,
        query_grads,
        block_maps,
        block_index,
        block_sign,
        ff_map,
    )
    other_feats = move(train_feats, "reps", lambda r: 1 - r)
    params = pltpu.CompilerParams(vmem_limit_bytes=VMEM_LIMIT)
    piece = jax.ShapeDtypeStruct((CHUNK, TILE), jnp.float32)
    keep, first, second, third = pl.pallas_call(
        gram_kernel,
        out_shape=[piece] * NY,
        scratch_shapes=[pltpu.VMEM((NY * CHUNK, TILE), jnp.float32)],
        compiler_params=params,
    )(train_feats, other_feats)
    second = along_y(second, 2)
    first = along_y(first, 1)
    third = along_y(third, 3)
    gram = keep + first + second + third
    held = jnp.concatenate([gram, query_feats], 0)
    near = move(held, "examples", lambda e: e ^ 1)
    held = jnp.concatenate([gram + near[:CHUNK], held[CHUNK:], near[CHUNK:]], 0)
    far = along_z(held, 4)
    left = along_z(held, 2)
    right = along_z(held, 6)
    gram = held[:CHUNK] + left[:CHUNK] + right[:CHUNK] + far[:CHUNK]
    held = jnp.concatenate([gram, held[CHUNK:], left[CHUNK:], right[CHUNK:], far[CHUNK:]], 0)
    second = along_y(held, 2)
    first = along_y(held, 1)
    third = along_y(held, 3)
    mine = [held, first, second, third]
    theirs = [move(piece, "reps", lambda r: 1 - r) for piece in mine]
    value = pl.pallas_call(
        solve_kernel,
        out_shape=jax.ShapeDtypeStruct((train_feats.shape[0], TILE), jnp.float32),
        scratch_shapes=[
            pltpu.VMEM((2 * NY * CHUNK, TILE), jnp.float32),
            pltpu.VMEM((KB, TILE), jnp.float32),
        ],
        compiler_params=params,
    )(*mine, *theirs, train_feats)
    second = move(value, "shard", lambda s: s ^ 2)
    first = move(value, "shard", lambda s: s ^ 1)
    third = move(value, "shard", lambda s: s ^ 3)
    return (value + first) + (second + third)


def solution(mesh):
    placed = (
        P(("examples", "reps"), None, None),
        P(("examples", "reps"), None, "shard"),
        P(("examples", "reps"), None, None),
        P(("examples", "reps"), None, "shard"),
        P(),
        P(),
        P(),
        P("shard", None),
    )
    return jax.shard_map(
        on_device,
        mesh=mesh,
        in_specs=placed,
        out_specs=P(("examples", "reps"), None),
        check_vma=False,
    )
```

```python
import math

import jax
import jax.numpy as jnp
from jax import lax
from jax.experimental import pallas as pl
from jax.experimental.pallas import tpu as pltpu
from jax.sharding import PartitionSpec as P

D = 4096
K1 = 32
K2 = 16
KB = 512
RANK = 8
EXAMPLES = 4096
NBLOCKS = 128
BLOCK_ROWS = 32
CHUNKS = 1
PARTS = 2
LATER = 8
RIDGE = 1.0
TILE = 128
PANEL = 16
NB = KB // TILE
NY = 4
NZ = 8
SIDES = [(0, 1), (0, 2), (0, 3)], [(1, 2), (1, 3), (2, 3)]
CHUNK = TILE + 8
HIGH = lax.Precision.HIGHEST
VMEM_LIMIT = 48 << 20
VMEM_WHOLE = 40 << 20


def dot(a, b, contract=(1, 0)):
    return lax.dot_general(
        a,
        b,
        (((contract[0],), (contract[1],)), ((), ())),
        precision=HIGH,
        preferred_element_type=jnp.float32,
    )


def short_dot(a, b):
    a_high, a_low, _ = split(a)
    b_high, b_low, _ = split(b)
    terms = ((a_low, b_high), (a_high, b_low), (a_high, b_high))
    return sum(jnp.dot(x, y, preferred_element_type=jnp.float32) for x, y in terms)


def move(block, axis, target):
    count = lax.axis_size(axis)
    return lax.ppermute(block, axis, [(i, target(i)) for i in range(count)])


def along_y(block, step):
    return move(block, "examples", lambda e: (e // NZ + step) % NY * NZ + e % NZ)


def along_z(block, step):
    return move(block, "examples", lambda e: e // NZ * NZ + (e % NZ + step) % NZ)


def split(value):
    high = value.astype(jnp.bfloat16)
    rest = value - high.astype(jnp.float32)
    middle = rest.astype(jnp.bfloat16)
    return high, middle, (rest - middle.astype(jnp.float32)).astype(jnp.bfloat16)


def spread_parts(value):
    high, middle, low = (part.astype(jnp.float32) for part in split(value))
    first = high + pltpu.roll(middle, 64, 1)
    return jnp.concatenate([first, low], 1).astype(jnp.bfloat16)


def feature_kernel(*refs):
    sources, feats_ref, query_ref = refs[:8], refs[8], refs[9]
    index_ref, sign_ref, maps_ref, ff_ref, grads_ref, inputs_ref = refs[10:16]
    dense, weights, ff_weights, total, right_total, arrived = refs[16:]
    index_hbm, sign_hbm, maps_hbm, ff_hbm, query_grads_hbm, grads_hbm, query_hbm, inputs_hbm = sources
    main = inputs_hbm.shape[0]
    rows = inputs_ref.shape[0]
    plan = [
        (index_hbm, index_ref),
        (sign_hbm, sign_ref),
        (ff_hbm, ff_ref),
        (maps_hbm, maps_ref),
        (query_grads_hbm, grads_ref.at[main:rows, :]),
        (grads_hbm, grads_ref.at[0:main, :]),
        (query_hbm, inputs_ref.at[main:rows, :]),
    ]
    width = inputs_ref.shape[1] // CHUNKS
    for k in range(CHUNKS):
        part = slice(k * width, (k + 1) * width)
        plan.append((inputs_hbm.at[:, part], inputs_ref.at[0:main, part]))
    copies = [
        pltpu.make_async_copy(source, target, arrived.at[k])
        for k, (source, target) in enumerate(plan)
    ]
    for copy in copies[:6]:
        copy.start()

    def iota(shape, axis):
        return lax.broadcasted_iota(jnp.int32, shape, axis)

    for copy in copies[:3]:
        copy.wait()
    place = (iota((K2, TILE), 1) - K1 == iota((K2, TILE), 0)).astype(jnp.bfloat16)
    ff_weights[...] = lax.dot_general(
        ff_ref[...], place, (((0,), (0,)), ((), ())), preferred_element_type=jnp.float32
    ).astype(jnp.bfloat16)

    copies[3].wait()
    signs = 2 * sign_ref[...] - 1
    chooser = [
        jnp.where(index_ref[...] == c, signs, 0).astype(jnp.float32) for c in range(K1 // K2)
    ]
    groups = TILE // K1
    group = iota((NBLOCKS, TILE), 1) // K1
    for first in range(0, BLOCK_ROWS, groups):
        if first == LATER:
            for copy in copies[6:]:
                copy.start()
        stack = []
        for i in range(first, first + groups):
            values = maps_ref[i].astype(jnp.float32)
            stack += [values * factor for factor in chooser]
        turned = jnp.concatenate(stack, 0).T
        for g in range(groups):
            dense[pl.ds(first + g, NBLOCKS, stride=BLOCK_ROWS), :] = jnp.where(
                group == g, turned, 0.0
            )
    weights[...] = dense[...].astype(jnp.bfloat16)

    def project(values_ref, weights_ref, out_ref):
        depth = values_ref.shape[1] // PARTS

        def body(k, carry):
            part = pl.ds(pl.multiple_of(k * depth, TILE), depth)
            out_ref[...] += jnp.dot(
                values_ref[:, part], weights_ref[part, :], preferred_element_type=jnp.float32
            )
            return carry

        out_ref[...] = jnp.zeros_like(out_ref)
        lax.fori_loop(0, PARTS, body, 0)

    copies[4].wait()
    copies[5].wait()
    project(grads_ref, ff_weights, right_total)
    for copy in copies[6:]:
        copy.wait()
    project(inputs_ref, weights, total)
    left = total[...]
    left = left + pltpu.roll(left, 2 * K1, 1)
    left = left + pltpu.roll(left, K1, 1)
    total[...] = jnp.where(iota((rows, TILE), 1) < K1, left, right_total[...])

    source = iota((2 * TILE, 2 * KB), 0) & 63
    lanes = iota((2 * TILE, 2 * KB), 1)
    from_left = (lanes < KB) & (source == lanes // K2)
    from_right = (lanes >= KB) & (source == K1 + (lanes & (K2 - 1)))
    used = iota((2 * TILE, 2 * KB), 0) < 3 * 64
    expand = ((from_left | from_right) & used).astype(jnp.bfloat16)
    count = feats_ref.shape[0]
    by_rank = [total[pl.ds(r, count, stride=RANK), :] for r in range(RANK)]
    by_rank.append(total[main:rows, :])
    wide = jnp.dot(
        spread_parts(jnp.concatenate(by_rank, 0)), expand, preferred_element_type=jnp.float32
    )
    product = wide[:, :KB] * wide[:, KB:]
    value = product[:count]
    for r in range(1, RANK):
        value = value + product[r * count : (r + 1) * count]
    feats_ref[...] = value * (1.0 / math.sqrt(RANK))
    for i in range((rows - main) // RANK):
        first = main + i * RANK
        row = jnp.sum(product[first : first + RANK], 0, keepdims=True) * (1.0 / math.sqrt(RANK))
        for c in range(NB):
            at = 2 * c + i
            query_ref[at : at + 1, :] = row[:, c * TILE : (c + 1) * TILE]


def features(train, grads, query, query_grads, block_maps, block_index, block_sign, ff_map):
    count = train.shape[0]
    train, grads, query, query_grads = (
        x.reshape(-1, x.shape[-1]) for x in (train, grads, query, query_grads)
    )
    operands = [
        block_index.reshape(1, -1),
        block_sign.reshape(1, -1),
        block_maps.transpose(1, 2, 0),
        ff_map.T,
        query_grads,
        grads,
        query,
        train,
    ]
    rows = train.shape[0] + query.shape[0]
    return pl.pallas_call(
        feature_kernel,
        in_specs=[pl.BlockSpec(memory_space=pltpu.HBM)] * len(operands),
        out_shape=[
            jax.ShapeDtypeStruct((count, KB), jnp.float32),
            jax.ShapeDtypeStruct((2 * NB, TILE), jnp.float32),
        ],
        scratch_shapes=[pltpu.VMEM(x.shape, x.dtype) for x in operands[:4]]
        + [
            pltpu.VMEM((rows, grads.shape[1]), jnp.bfloat16),
            pltpu.VMEM((rows, D), jnp.bfloat16),
            pltpu.VMEM((D, TILE), jnp.float32),
            pltpu.VMEM((D, TILE), jnp.bfloat16),
            pltpu.VMEM((grads.shape[1], TILE), jnp.bfloat16),
            pltpu.VMEM((rows, TILE), jnp.float32),
            pltpu.VMEM((rows, TILE), jnp.float32),
            pltpu.SemaphoreType.DMA((7 + CHUNKS,)),
        ],
        compiler_params=pltpu.CompilerParams(vmem_limit_bytes=VMEM_WHOLE),
    )(*[pltpu.with_memory_space_constraint(x, pltpu.HBM) for x in operands])


def gram_kernel(own_ref, other_ref, keep_ref, first_ref, second_ref, third_ref, half):
    rep = lax.axis_index("reps")
    y = lax.axis_index("examples") // NZ

    def product(low, high):
        row = pl.multiple_of(jnp.where(rep == 0, low[0], high[0]) * TILE, TILE)
        col = pl.multiple_of(jnp.where(rep == 0, low[1], high[1]) * TILE, TILE)
        total = dot(own_ref[:, pl.ds(row, TILE)], own_ref[:, pl.ds(col, TILE)], (0, 0))
        total += dot(other_ref[:, pl.ds(row, TILE)], other_ref[:, pl.ds(col, TILE)], (0, 0))
        return total * (1.0 / EXAMPLES)

    row = lax.broadcasted_iota(jnp.int32, (TILE, TILE), 0)
    col = lax.broadcasted_iota(jnp.int32, (TILE, TILE), 1)
    upper, lower = product((0, 0), (2, 2)), product((1, 1), (3, 3))
    half[...] = jnp.zeros_like(half)
    half[:TILE, :] = jnp.where(row <= col, upper, lower)
    half[TILE : TILE + 1, :] = jnp.sum(jnp.where(row == col, lower, 0.0), 0, keepdims=True)
    for place, (low, high) in enumerate(zip(*SIDES), 1):
        half[place * CHUNK : place * CHUNK + TILE, :] = product(low, high)
    for step, out_ref in enumerate((keep_ref, first_ref, second_ref, third_ref)):
        start = pl.multiple_of(lax.rem(y + step, NY) * CHUNK, 8)
        out_ref[...] = half[pl.ds(start, CHUNK), :]


def panel_inverse(rows, first):
    lane = lax.broadcasted_iota(jnp.int32, (PANEL, TILE), 1)
    row = lax.broadcasted_iota(jnp.int32, (PANEL, TILE), 0)
    spread = [
        jnp.broadcast_to(rows[:, first + j : first + j + 1], (PANEL, TILE)) for j in range(PANEL)
    ]
    inside = (lane >= first) & (lane < first + PANEL)
    rows = jnp.where(inside, (lane - first == row).astype(jnp.float32), rows)
    for j in range(PANEL):
        scale = 1.0 / spread[j][j : j + 1, :]
        pivot_row = rows[j : j + 1, :] * scale
        rows = jnp.where(row == j, pivot_row, rows - spread[j] * pivot_row)
        for k in range(j + 1, PANEL):
            part = spread[k][j : j + 1, :] * scale
            spread[k] = jnp.where(row == j, part, spread[k] - spread[j] * part)
    return rows


def panel_update(rows, factors, first, fresh):
    lane = lax.broadcasted_iota(jnp.int32, (PANEL, TILE), 1)
    inside = (lane >= first) & (lane < first + PANEL)
    even, odd = jnp.where(inside, 0.0, rows), None
    for j in range(PANEL):
        column = jnp.broadcast_to(factors[:, first + j : first + j + 1], (PANEL, TILE))
        term = column * fresh[j : j + 1]
        if j % 2 == 0:
            even = even - term
        else:
            odd = term if odd is None else odd + term
    return even - odd


def block_inverse(block, between=lambda: None):
    lane = lax.broadcasted_iota(jnp.int32, (PANEL, TILE), 1)
    count = TILE // PANEL
    rows = [block[i * PANEL : (i + 1) * PANEL] for i in range(count)]
    fresh = None
    for t in range(count):
        first = t * PANEL
        current = rows[t]
        if t:
            current = panel_update(current, current, first - PANEL, fresh)
        fresh = panel_inverse(current, first)
        others = [i for i in range(count) if i not in (t, t + 1)]
        factors = jnp.concatenate([rows[i] for i in others], 0)[:, first : first + PANEL]
        update = dot(factors, fresh)
        inside = (lane >= first) & (lane < first + PANEL)
        for k, i in enumerate(others):
            rows[i] = jnp.where(inside, 0.0, rows[i]) - update[k * PANEL : (k + 1) * PANEL]
        rows[t] = fresh
        between()
    return jnp.concatenate(rows, 0)


def solve_kernel(*refs):
    pieces, (feats_ref, out_ref, gram, query) = refs[: 2 * NY], refs[2 * NY :]
    rep = lax.axis_index("reps")
    spot = lax.axis_index("examples")
    y, z = spot // NZ, lax.rem(spot, NZ)
    query_rows = pieces[0].shape[0] - CHUNK
    for place, ref in enumerate(pieces):
        holder = rep if place < NY else 1 - rep
        source = lax.rem(y + NY - place % NY, NY)
        start = pl.multiple_of((holder * NY + source) * CHUNK, 8)
        gram[pl.ds(start, CHUNK), :] = ref[:CHUNK, :]
        query[place * query_rows : (place + 1) * query_rows, :] = ref[CHUNK:, :]

    total_rows = 2 * NY * query_rows
    r = lax.broadcasted_iota(jnp.int32, (total_rows, TILE), 0)
    n = lax.broadcasted_iota(jnp.int32, (total_rows, TILE), 1)
    side, step = r >> 8, (r >> 6) & 3
    group, pair, part, item = (r >> 4) & 3, (r >> 3) & 1, (r >> 1) & 3, r & 1
    shift = jnp.where(group == 0, 0, jnp.where(group == 1, 6, jnp.where(group == 2, 2, 4)))
    source_z = ((z + shift) & 7) ^ pair
    source_y = (y + 4 - step) & 3
    source = (((source_y * NZ + source_z) * 2 + (side ^ rep)) * 2) + item
    right = [None] * NB

    def pick(c):
        chosen = ((source == n) & (part == c)).astype(jnp.bfloat16)
        right[c] = sum(
            lax.dot_general(
                piece, chosen, (((0,), (0,)), ((), ())), preferred_element_type=jnp.float32
            )
            for piece in split(query[...])
        )

    row = lax.broadcasted_iota(jnp.int32, (TILE, TILE), 0)
    col = lax.broadcasted_iota(jnp.int32, (TILE, TILE), 1)
    ridge = jnp.where(row == col, RIDGE, 0.0)
    block = {}
    for core, pairs in enumerate(SIDES):
        first = core * NY * CHUNK
        packed = gram[first : first + TILE, :]
        above = jnp.where(row < col, packed, 0.0)
        block[2 * core, 2 * core] = jnp.where(row <= col, packed, above.T) + ridge
        below = jnp.where(row > col, packed, 0.0)
        diagonal = gram[first + TILE : first + TILE + 1, :]
        other = jnp.where(row > col, packed, jnp.where(row == col, diagonal, below.T))
        block[2 * core + 1, 2 * core + 1] = other + ridge
        for place, pair in enumerate(pairs, 1):
            start = first + place * CHUNK
            block[pair] = gram[start : start + TILE, :]

    solved = []
    pending = [lambda c=c: pick(c) for c in range(NB)]

    def between():
        if pending:
            pending.pop(0)()

    turned = {}

    def turn(b):
        turned[b] = block[b, b + 1].T

    for b in range(NB):
        if b < NB - 1:
            pending.append(lambda b=b: turn(b))
        inverse = block_inverse(block[b, b], between)
        while pending:
            between()
        if b == NB - 1:
            solved.append([dot(inverse, right[b])])
            break
        near = dot(inverse, block[b, b + 1])
        block[b + 1, b + 1] = block[b + 1, b + 1] - dot(turned[b], near)
        done = [near]
        solved.append(done)

        def finish(b=b, done=done, inverse=inverse):
            width = NB - 2 - b
            wide = jnp.concatenate([block[b, j] for j in range(b + 2, NB)] + [right[b]], 1)
            wide = dot(inverse, wide)
            done += [wide[:, k * TILE : (k + 1) * TILE] for k in range(width + 1)]

        def trail(i, b=b, done=done):
            first = max(i, b + 2)
            change = dot(block[b, i], jnp.concatenate(done[first - b - 1 :], 1), (0, 0))
            for j in range(first, NB):
                at = (j - first) * TILE
                block[i, j] = block[i, j] - change[:, at : at + TILE]
            right[i] = right[i] - change[:, (NB - first) * TILE :]

        pending.append(finish)
        for i in range(b + 1, NB):
            pending.append(lambda i=i, trail=trail: trail(i))
    answer = [None] * NB
    for b in reversed(range(NB)):
        value = solved[b][NB - 1 - b]
        if b < NB - 1:
            later = jnp.concatenate(answer[b + 1 :], 0)
            value = value - short_dot(jnp.concatenate(solved[b][: NB - 1 - b], 1), later)
        answer[b] = value
    out_ref[...] = short_dot(feats_ref[...], jnp.concatenate(answer, 0)) * (1.0 / math.sqrt(4 * KB))


def on_device(
    train_inputs,
    train_grads,
    query_inputs,
    query_grads,
    block_maps,
    block_index,
    block_sign,
    ff_map,
):
    train_feats, query_feats = features(
        train_inputs,
        train_grads,
        query_inputs,
        query_grads,
        block_maps,
        block_index,
        block_sign,
        ff_map,
    )
    other_feats = move(train_feats, "reps", lambda r: 1 - r)
    params = pltpu.CompilerParams(vmem_limit_bytes=VMEM_LIMIT)
    piece = jax.ShapeDtypeStruct((CHUNK, TILE), jnp.float32)
    keep, first, second, third = pl.pallas_call(
        gram_kernel,
        out_shape=[piece] * NY,
        scratch_shapes=[pltpu.VMEM((NY * CHUNK, TILE), jnp.float32)],
        compiler_params=params,
    )(train_feats, other_feats)
    second = along_y(second, 2)
    first = along_y(first, 1)
    third = along_y(third, 3)
    gram = keep + first + second + third
    held = jnp.concatenate([gram, query_feats], 0)
    near = move(held, "examples", lambda e: e ^ 1)
    held = jnp.concatenate([gram + near[:CHUNK], held[CHUNK:], near[CHUNK:]], 0)
    far = along_z(held, 4)
    left = along_z(held, 2)
    right = along_z(held, 6)
    gram = held[:CHUNK] + left[:CHUNK] + right[:CHUNK] + far[:CHUNK]
    held = jnp.concatenate([gram, held[CHUNK:], left[CHUNK:], right[CHUNK:], far[CHUNK:]], 0)
    second = along_y(held, 2)
    first = along_y(held, 1)
    third = along_y(held, 3)
    mine = [held, first, second, third]
    theirs = [move(piece, "reps", lambda r: 1 - r) for piece in mine]
    value = pl.pallas_call(
        solve_kernel,
        out_shape=jax.ShapeDtypeStruct((train_feats.shape[0], TILE), jnp.float32),
        scratch_shapes=[
            pltpu.VMEM((2 * NY * CHUNK, TILE), jnp.float32),
            pltpu.VMEM((KB, TILE), jnp.float32),
        ],
        compiler_params=params,
    )(*mine, *theirs, train_feats)
    second = move(value, "shard", lambda s: s ^ 2)
    first = move(value, "shard", lambda s: s ^ 1)
    third = move(value, "shard", lambda s: s ^ 3)
    return (value + first) + (second + third)


def solution(mesh):
    placed = (
        P(("examples", "reps"), None, None),
        P(("examples", "reps"), None, "shard"),
        P(("examples", "reps"), None, None),
        P(("examples", "reps"), None, "shard"),
        P(),
        P(),
        P(),
        P("shard", None),
    )
    return jax.shard_map(
        on_device,
        mesh=mesh,
        in_specs=placed,
        out_specs=P(("examples", "reps"), None),
        check_vma=False,
    )
```
